32 devices in a mesh: ctx: 8 (over z, x), head: 4 (over y, core).
Axes of the slice: x: 2, y: 2, z: 4, core: 2. Of those that a mesh axis runs over, the one named last changes fastest.
Arguments:
- queries: bfloat16 [2048, 64, 128], P('ctx', 'head'), may hold values from -16 to 16
- keys: bfloat16 [2048, 8, 128], P(('ctx', 'head')), may hold values from -8 to 8
- values: bfloat16 [2048, 8, 128], P(('ctx', 'head')), may hold values from -6 to 6
- grad_out: bfloat16 [2048, 64, 128], P('ctx', 'head'), may hold values from -6 to 6
- lengths: int32 [8], replicated, may hold values from 1 to 768, 2048 in all
Outputs:
- attended: bfloat16 [2048, 64, 128], P('ctx', 'head')
- d_queries: bfloat16 [2048, 64, 128], P('ctx', 'head')
- d_keys: bfloat16 [2048, 8, 128], P(('ctx', 'head'))
- d_values: bfloat16 [2048, 8, 128], P(('ctx', 'head'))
The draws below stay inside these ranges and needn't reach their ends.
Inputs may be any that keep to these rules, and one draw needn't show every extreme that they name: `lengths`: the 8 documents fill the window; the longest has exactly 768 tokens.
All inputs are finite; a program needn't handle non-finite values.
Results may differ from the reference program's by a relative error of at most 0.0085.
Values may be sent and summed in bfloat16 or wider, within the bound.
No kernel may reach another device: no remote copies, remote signals or barrier semaphores. Data moves between devices by JAX's collectives and lax.ppermute only.
A program may use at most 64 MiB of HBM per device.

```python
import math
import jax
import jax.numpy as jnp
import numpy as np
from jax import lax

D_HEAD = 128
Q_HEADS = 64
KV_HEADS = 8
TOK_DEV = 256
BACK = 3
TOKENS = 2048
MOST = 768
DOCS = 8
N_CTX = 8


def draw_queries(key, part):
    base_key = jax.random.fold_in(jax.random.fold_in(key, 17), 0)
    entries = jnp.clip(jax.random.normal(base_key, (TOKENS, Q_HEADS, D_HEAD), jnp.float32), -4.0, 4.0)
    return entries.astype(jnp.bfloat16)


def draw_keys(key, part):
    base_key = jax.random.fold_in(jax.random.fold_in(key, 23), 0)
    entries = jnp.clip(jax.random.normal(base_key, (TOKENS, KV_HEADS, D_HEAD), jnp.float32), -4.0, 4.0)
    return entries.astype(jnp.bfloat16)


def block_scale(own_key, extent, cuts, low, largest):
    level = 1.0
    for axis_at, parts in cuts:
        draws = jax.random.uniform(jax.random.fold_in(jax.random.fold_in(own_key, 6), axis_at), (parts,), jnp.float32, low / len(cuts), largest / len(cuts))
        level = level * jnp.repeat(jnp.exp(draws), extent[axis_at] // parts).reshape((-1,) + (1,) * (len(extent) - 1 - axis_at))
    return level


def split_up(number_of, total, most, lean):
    loads = [(1 << 20) // math.isqrt(rank ** lean) + 1 for rank in range(2, number_of + 1)]
    spare, holding = total - most - (number_of - 1), [1] * (number_of - 1)
    while spare > 0:
        movable = [i for i in range(number_of - 1) if holding[i] < most]
        whole, budget = sum([loads[i] for i in movable]), spare
        for i in movable:
            addition = min(most - holding[i], max(1, budget * loads[i] // whole), spare)
            holding[i] = holding[i] + addition
            spare = spare - addition
    return np.array([most] + holding)


def ragged(rng, number_of, total, reach, slope):
    if number_of == 2:
        one = jax.random.randint(rng, (), max(1, total - reach), min(reach, total - 1) + 1)
        return jnp.stack([one, total - one])
    sizes = jnp.asarray(split_up(number_of, total, reach, slope), jnp.int32)
    twos = (number_of - 1) // 2
    donor, receiver = sizes[1:1 + 2 * twos:2], sizes[2:2 + 2 * twos:2]
    slack = jnp.minimum(donor - 1, reach - receiver)
    moved = jax.random.randint(jax.random.fold_in(rng, 1), (twos,), 0, 1 << 20) % (slack + 1)
    sizes = sizes.at[1:1 + 2 * twos:2].set(donor - moved).at[2:2 + 2 * twos:2].set(receiver + moved)
    return sizes[jax.random.permutation(jax.random.fold_in(rng, 2), number_of)]


def scatter_about(rng, dims, scale, most, shards=(), kind=jnp.bfloat16):
    result = scale * jax.random.normal(rng, dims, jnp.float32)
    if shards:
        result = result * block_scale(rng, dims, shards, -0.22, 0.18)
    return jnp.clip(result, -most, most).astype(kind)


def setup_inputs(seed: int = 0) -> dict:
    streams_of = jax.random.split(jax.random.key(seed), 6)
    queries = draw_queries(jax.random.fold_in(streams_of[5], 71), 0)
    keys = draw_keys(jax.random.fold_in(streams_of[5], 71), 0)
    values = scatter_about(streams_of[2], (TOKENS, KV_HEADS, D_HEAD), 1.0, 6.0, ((0, 32),))
    grad_out = scatter_about(streams_of[3], (TOKENS, Q_HEADS, D_HEAD), 1.0, 6.0, ((0, 8), (1, 4)))
    lengths = ragged(streams_of[4], DOCS, TOKENS, MOST, 2).astype(jnp.int32)
    return {"queries": queries, "keys": keys, "values": values, "grad_out": grad_out, "lengths": lengths}


def head_pass(query_rows, grad_rows, key_rows, value_rows, allowed):
    inv_root = query_rows.shape[-1] ** -0.5
    scores = jnp.dot(query_rows, key_rows.T, preferred_element_type=jnp.float32) * inv_root
    masked = jnp.where(allowed, scores, -jnp.inf)
    top_score = jnp.max(masked, axis=1, keepdims=True)
    log_total = top_score + jnp.log(jnp.sum(jnp.exp(masked - top_score), axis=1, keepdims=True))
    probs = jnp.exp(masked - log_total)
    probs_low = probs.astype(jnp.bfloat16)
    attended = jnp.dot(probs_low, value_rows, preferred_element_type=jnp.float32).astype(jnp.bfloat16)
    correction = jnp.sum(grad_rows.astype(jnp.float32) * attended.astype(jnp.float32), axis=1, keepdims=True)
    grad_probs = jnp.dot(grad_rows, value_rows.T, preferred_element_type=jnp.float32)
    grad_scores = (probs * (grad_probs - correction)).astype(jnp.bfloat16)
    grad_values = jnp.dot(probs_low.T, grad_rows, preferred_element_type=jnp.float32)
    grad_query = (jnp.dot(grad_scores, key_rows, preferred_element_type=jnp.float32) * inv_root).astype(jnp.bfloat16)
    grad_keys = jnp.dot(grad_scores.T, query_rows, preferred_element_type=jnp.float32) * inv_root
    return attended, grad_query, grad_keys, grad_values


def group_pass(query_group, grad_group, key_rows, value_rows, allowed):
    def one_head(head_inputs):
        return head_pass(head_inputs[0], head_inputs[1], key_rows, value_rows, allowed)

    attended, grad_query, grad_keys, grad_values = lax.map(
        one_head, (jnp.moveaxis(query_group, 1, 0), jnp.moveaxis(grad_group, 1, 0)))
    return (jnp.moveaxis(attended, 0, 1), jnp.moveaxis(grad_query, 0, 1),
            jnp.sum(grad_keys, axis=0), jnp.sum(grad_values, axis=0))


def attend(query_split, grad_split, key_span, value_span, allowed):
    results = [group_pass(query_split[:, group], grad_split[:, group], key_span[:, group], value_span[:, group], allowed)
               for group in range(query_split.shape[1])]
    return tuple(jnp.stack([member[slot_index] for member in results], axis=1) for slot_index in range(4))


def doc_start(starts, positions):
    return jnp.max(jnp.where(starts[None, :] <= positions[:, None], starts[None, :], 0), axis=1)


def reference(queries, keys, values, grad_out, lengths):
    kv_heads = keys.shape[1]
    head_dim = keys.shape[2]
    per_group = queries.shape[1] // kv_heads
    span_rows = (BACK + 1) * TOK_DEV
    starts = (jnp.cumsum(lengths) - lengths).astype(jnp.int32)
    leading = jnp.zeros((BACK * TOK_DEV, kv_heads, head_dim), keys.dtype)
    key_padded = jnp.concatenate([leading, keys], axis=0)
    value_padded = jnp.concatenate([leading, values], axis=0)

    def one_block(block_index):
        offset = (block_index * TOK_DEV).astype(jnp.int32)
        query_split = lax.dynamic_slice_in_dim(queries, offset, TOK_DEV, 0).reshape(TOK_DEV, kv_heads, per_group, head_dim)
        grad_split = lax.dynamic_slice_in_dim(grad_out, offset, TOK_DEV, 0).reshape(TOK_DEV, kv_heads, per_group, head_dim)
        key_span = lax.dynamic_slice_in_dim(key_padded, offset, span_rows, 0)
        value_span = lax.dynamic_slice_in_dim(value_padded, offset, span_rows, 0)
        query_pos = offset + jnp.arange(TOK_DEV, dtype=jnp.int32)
        key_pos = offset - BACK * TOK_DEV + jnp.arange(span_rows, dtype=jnp.int32)
        query_start = doc_start(starts, query_pos)
        allowed = (key_pos[None, :] >= query_start[:, None]) & (key_pos[None, :] <= query_pos[:, None])
        return attend(query_split, grad_split, key_span, value_span, allowed)

    attended, grad_query, grad_keys, grad_values = lax.map(one_block, jnp.arange(N_CTX, dtype=jnp.int32))
    key_parts = grad_keys.reshape(N_CTX, BACK + 1, TOK_DEV, kv_heads, head_dim)
    value_parts = grad_values.reshape(N_CTX, BACK + 1, TOK_DEV, kv_heads, head_dim)
    key_total = jnp.zeros((N_CTX + BACK, TOK_DEV, kv_heads, head_dim), jnp.float32)
    value_total = jnp.zeros((N_CTX + BACK, TOK_DEV, kv_heads, head_dim), jnp.float32)
    for slot_index in range(BACK + 1):
        key_total = key_total.at[slot_index:slot_index + N_CTX].add(key_parts[:, slot_index])
        value_total = value_total.at[slot_index:slot_index + N_CTX].add(value_parts[:, slot_index])
    d_keys = key_total[BACK:].reshape(TOKENS, kv_heads, head_dim).astype(jnp.bfloat16)
    d_values = value_total[BACK:].reshape(TOKENS, kv_heads, head_dim).astype(jnp.bfloat16)
    attended = attended.reshape(TOKENS, Q_HEADS, head_dim)
    d_queries = grad_query.reshape(TOKENS, Q_HEADS, head_dim)
    return attended, d_queries, d_keys, d_values
```

```python
import functools
import math
import jax
import jax.numpy as jnp
from jax import lax
from jax.experimental import pallas as pl
from jax.experimental.pallas import tpu as pltpu
from jax.sharding import PartitionSpec as P

BACK = 3
LANE = 128
F32 = jnp.float32
BF16 = jnp.bfloat16
NEG = -1e30


def _dot(a, b, ca, cb):
    return lax.dot_general(a, b, (((ca,), (cb,)), ((), ())), preferred_element_type=F32)


def attention_kernel(tok, part, per_group, chunk, windows, lengths_ref, shard_ref, q_ref, g_ref, *refs):
    spans, refs = refs[:BACK + 1], refs[BACK + 1:]
    before, refs = refs[:2 * part], refs[2 * part:]
    att_ref, dq_ref = refs[:2]
    d_refs = refs[2:3 + BACK]
    k_sc, v_sc, kt_sc, vt_sc, dk_sc, dv_sc = refs[3 + BACK:]
    block, heads, head = q_ref.shape
    rows = chunk * per_group
    subs = range(block // chunk)
    scale = head ** -0.5
    c2 = scale * math.log2(math.e)
    step = pl.program_id(0)
    base = shard_ref[0] * tok
    span0 = base - BACK * tok
    docs = lengths_ref.shape[0]

    @pl.when(step == 0)
    def _():
        for i, kv in enumerate(reversed(spans)):
            at = pl.ds(i * tok, tok)
            k = kv[0]
            v = kv[1]
            k_sc[at, :] = k
            v_sc[at, :] = v
            kt_sc[:, at] = k.T
            vt_sc[:, at] = v.T
        dk_sc[...] = jnp.zeros_like(dk_sc)
        dv_sc[...] = jnp.zeros_like(dv_sc)

    p0 = base + step * block
    pos = [p0 + s * chunk - span0 + lax.broadcasted_iota(jnp.int32, (1, rows), 1) // per_group for s in subs]

    def add_doc(d, carry):
        begin, first, vecs = carry
        at = begin - span0
        first = jnp.where(begin <= p0, at, first)
        vecs = tuple(jnp.where(at <= pos[s], at, vecs[s]) for s in subs)
        return begin + lengths_ref[d], first, vecs

    none = jnp.zeros((1, rows), jnp.int32)
    _, first, start = lax.fori_loop(0, docs, add_doc, (jnp.int32(0), jnp.int32(0), (none,) * len(subs)))
    top = BACK * tok + (step + 1) * block
    need = top - first

    def mine(ref):
        wide = ref[...].astype(F32)[:, part * per_group:(part + 1) * per_group, :]
        return [wide[s * chunk:(s + 1) * chunk].reshape(rows, head).astype(BF16) for s in subs]

    def body(width):
        low = pl.multiple_of(top - width, LANE)
        wide = [width - (len(subs) - 1 - s) * chunk for s in subs]
        at = [pl.ds(low, w) for w in wide]
        q, go = mine(q_ref), mine(g_ref)
        s = [_dot(k_sc[at[i], :], q[i], 1, 1) for i in subs]
        dp = [_dot(v_sc[at[i], :], go[i], 1, 1) for i in subs]
        masked = []
        for i in subs:
            w = wide[i]
            key = low + lax.broadcasted_iota(jnp.int32, (w, rows), 0)
            x = jnp.where(key >= start[i], s[i], NEG)
            end = jnp.where(key[w - chunk:] <= pos[i], x[w - chunk:], NEG)
            masked.append(jnp.concatenate([x[:w - chunk], end], 0) if w > chunk else end)
        m = [jnp.max(x, axis=0, keepdims=True) * c2 for x in masked]
        e = [jnp.exp2(masked[i] * c2 - m[i]) for i in subs]
        inv = [1.0 / jnp.sum(x, axis=0, keepdims=True) for x in e]
        p = [e[i] * inv[i] for i in subs]
        corr = [jnp.sum(p[i] * dp[i], axis=0, keepdims=True) for i in subs]
        pb = [x.astype(BF16) for x in p]
        ds = [(p[i] * (dp[i] - corr[i])).astype(BF16) for i in subs]
        ot = [_dot(vt_sc[:, pl.ds(low, width)][:, :wide[i]], pb[i], 1, 0).astype(BF16) for i in subs]
        dqt = [(_dot(kt_sc[:, pl.ds(low, width)][:, :wide[i]], ds[i], 1, 0) * scale).astype(BF16) for i in subs]
        for i in subs:
            dv_sc[at[i], :] += _dot(pb[i], go[i], 1, 0)
            dk_sc[at[i], :] += _dot(ds[i], q[i], 1, 0)
        for n, (out, cols) in enumerate(((att_ref, ot), (dq_ref, dqt))):
            for i in subs:
                new = cols[i].T
                if len(out.shape) == 2:
                    out[i * rows:(i + 1) * rows, :] = new
                    continue
                earlier = [before[2 * j + n][i * rows:(i + 1) * rows, :] for j in range(part)]
                both = [x.astype(F32).reshape(chunk, per_group, head) for x in (*earlier, new)]
                both = jnp.concatenate(both, 1) if len(both) > 1 else both[0]
                out[i * chunk:(i + 1) * chunk] = both.astype(BF16)

    for n, width in enumerate(windows):
        cond = need <= width
        if n:
            cond &= need > windows[n - 1]
        pl.when(cond)(functools.partial(body, width))

    @pl.when(step == pl.num_programs(0) - 1)
    def _():
        for i, out in enumerate(reversed(d_refs)):
            at = pl.ds(i * tok, tok)
            out[0] = (dk_sc[at, :] * scale).astype(out.dtype)
            out[1] = dv_sc[at, :].astype(out.dtype)


def attention(queries, grad_out, kvs, lengths, shard, part, parts, before, block=LANE, chunk=32):
    tok, heads, head = queries.shape
    per_group = heads // parts
    span = (BACK + 1) * tok
    most = BACK * tok + block
    windows = tuple(range(LANE, most + 1, LANE))
    rows = block * per_group
    smem = pl.BlockSpec(memory_space=pltpu.SMEM)
    whole = pl.BlockSpec((2, tok, head), lambda i: (0, 0, 0))
    tall = pl.BlockSpec((block, heads, head), lambda i: (i, 0, 0))
    flat = pl.BlockSpec((rows, head), lambda i: (i, 0))
    last = part == parts - 1
    out = jax.ShapeDtypeStruct(queries.shape if last else (tok * per_group, head), BF16)
    share = jax.ShapeDtypeStruct((2, tok, head), BF16)
    own = jax.ShapeDtypeStruct((2, tok, head), F32)
    return pl.pallas_call(
        functools.partial(attention_kernel, tok, part, per_group, chunk, windows),
        grid=(tok // block,),
        out_shape=(out, out, own) + (share,) * BACK,
        in_specs=[smem, smem, tall, tall] + [whole] * (BACK + 1) + [flat] * (2 * part),
        out_specs=(tall if last else flat,) * 2 + (whole,) * (BACK + 1),
        scratch_shapes=[
            pltpu.VMEM((span, head), BF16),
            pltpu.VMEM((span, head), BF16),
            pltpu.VMEM((head, span), BF16),
            pltpu.VMEM((head, span), BF16),
            pltpu.VMEM((span, head), F32),
            pltpu.VMEM((span, head), F32),
        ],
        compiler_params=pltpu.CompilerParams(
            dimension_semantics=("arbitrary",), vmem_limit_bytes=40 * 2**20),
        cost_estimate=pl.CostEstimate(
            flops=12 * tok * per_group * 2 * tok * head, bytes_accessed=4 * tok * heads * head * 2, transcendentals=0),
        name="attention",
    )(lengths, shard, queries, grad_out, *kvs, *before)


def turn(block, distance):
    n = lax.axis_size("ctx")
    return lax.ppermute(block, "ctx", [(i, (i + distance) % n) for i in range(n)])


def swap(block):
    return lax.ppermute(block, "ctx", [(i, i ^ 1) for i in range(lax.axis_size("ctx"))])


def relay(block, distance):
    n = lax.axis_size("ctx")
    return lax.ppermute(block, "ctx", [(i, i + distance) for i in range(0, n, 2) if 0 <= i + distance < n])


def on_device(queries, keys, values, grad_out, lengths):
    n_head = lax.axis_size("head")
    few, kv_heads, head = keys.shape
    parts = kv_heads // n_head
    tok = queries.shape[0]
    shard = lax.axis_index("ctx").astype(jnp.int32)
    odd = shard % 2 == 1
    both = jnp.stack([keys, values]).reshape(2, few, n_head, parts, head).transpose(2, 3, 0, 1, 4)
    both = lax.all_to_all(both, "head", 0, 0, tiled=True)
    own = [both[:, p].transpose(1, 0, 2, 3).reshape(2, tok, head) for p in range(parts)]
    two = [turn(x, 2) for x in own]
    pair = [swap(x) for x in own]
    three = [turn(x, 1) for x in two]
    one = [jnp.where(odd, x, relay(x, 2)) for x in pair]
    before, totals = [], []
    for p in range(parts):
        attended, d_queries, g0, g1, g2, g3 = attention(
            queries, grad_out, (own[p], one[p], two[p], three[p]), lengths, shard.reshape(1), p, parts, before)
        before += [attended, d_queries]
        back3 = turn(g3, -1)
        back1 = relay(g1, -2)
        back2 = turn((g2.astype(F32) + back3.astype(F32)).astype(BF16), -2)
        back_pair = swap(jnp.where(odd, g1, back1))
        totals.append((g0 + back2.astype(F32) + back_pair.astype(F32)).astype(BF16))
    total = jnp.stack(totals).reshape(parts, 2, n_head, few, head).transpose(2, 1, 3, 0, 4)
    total = lax.all_to_all(total, "head", 0, 0, tiled=True)
    done = total.transpose(1, 2, 0, 3, 4).reshape(2, few, kv_heads, head)
    return attended, d_queries, done[0], done[1]


def solution(mesh):
    split = P("ctx", "head", None)
    fine = P(("ctx", "head"), None, None)
    return jax.shard_map(
        on_device,
        mesh=mesh,
        in_specs=(split, fine, fine, split, P()),
        out_specs=(split, split, fine, fine),
        check_vma=False,
    )
```

```python
import functools
import math
import jax
import jax.numpy as jnp
from jax import lax
from jax.experimental import pallas as pl
from jax.experimental.pallas import tpu as pltpu
from jax.sharding import PartitionSpec as P

BACK = 3
LANE = 128
F32 = jnp.float32
BF16 = jnp.bfloat16
NEG = -1e30


def _dot(a, b, ca, cb):
    return lax.dot_general(a, b, (((ca,), (cb,)), ((), ())), preferred_element_type=F32)


def attention_kernel(tok, few, chunk, windows, lengths_ref, place_ref, q_ref, g_ref, *refs):
    spans, refs = refs[:BACK + 1], refs[BACK + 1:]
    (att_ref, dq_ref), d_refs = refs[:2], refs[2:3 + BACK]
    k_sc, v_sc, kt_sc, vt_sc, dk_sc, dv_sc = refs[3 + BACK:]
    block, heads, head = q_ref.shape
    groups = k_sc.shape[0]
    per_group = heads // groups
    rows = chunk * per_group
    subs = range(block // chunk)
    scale = head ** -0.5
    c2 = scale * math.log2(math.e)
    step = pl.program_id(0)
    base = place_ref[0] * tok
    span0 = base - BACK * tok
    docs = lengths_ref.shape[0]

    def place(i, s):
        return pl.ds(pl.multiple_of(i * tok + (place_ref[1] ^ s) * few, few), few)

    @pl.when(step == 0)
    def _():
        for i, kv in enumerate(reversed(spans)):
            for g in range(groups):
                lanes = slice(g * head, (g + 1) * head)
                for s in range(tok // few):
                    part = slice(s * few, (s + 1) * few)
                    k_sc[g, place(i, s), :] = kv[0, part, lanes]
                    v_sc[g, place(i, s), :] = kv[1, part, lanes]
                at = pl.ds(i * tok, tok)
                kt_sc[g, :, at] = k_sc[g, at, :].T
                vt_sc[g, :, at] = v_sc[g, at, :].T
        dk_sc[...] = jnp.zeros_like(dk_sc)
        dv_sc[...] = jnp.zeros_like(dv_sc)

    p0 = base + step * block
    pos = [p0 + s * chunk - span0 + lax.broadcasted_iota(jnp.int32, (1, rows), 1) // per_group for s in subs]

    def add_doc(d, carry):
        begin, first, vecs = carry
        at = begin - span0
        first = jnp.where(begin <= p0, at, first)
        vecs = tuple(jnp.where(at <= pos[s], at, vecs[s]) for s in subs)
        return begin + lengths_ref[d], first, vecs

    none = jnp.zeros((1, rows), jnp.int32)
    _, first, start = lax.fori_loop(0, docs, add_doc, (jnp.int32(0), jnp.int32(0), (none,) * len(subs)))
    top = BACK * tok + (step + 1) * block
    need = top - first

    def mine(ref, g):
        wide = ref[...].astype(F32)[:, g * per_group:(g + 1) * per_group, :]
        return [wide[s * chunk:(s + 1) * chunk].reshape(rows, head).astype(BF16) for s in subs]

    def one_group(g, low, width):
        wide = [width - (len(subs) - 1 - s) * chunk for s in subs]
        at = [pl.ds(low, w) for w in wide]
        q, go = mine(q_ref, g), mine(g_ref, g)
        s = [_dot(k_sc[g, at[i], :], q[i], 1, 1) for i in subs]
        dp = [_dot(v_sc[g, at[i], :], go[i], 1, 1) for i in subs]
        masked = []
        for i in subs:
            w = wide[i]
            key = low + lax.broadcasted_iota(jnp.int32, (w, rows), 0)
            x = jnp.where(key >= start[i], s[i], NEG)
            end = jnp.where(key[w - chunk:] <= pos[i], x[w - chunk:], NEG)
            masked.append(jnp.concatenate([x[:w - chunk], end], 0) if w > chunk else end)
        m = [jnp.max(x, axis=0, keepdims=True) * c2 for x in masked]
        e = [jnp.exp2(masked[i] * c2 - m[i]) for i in subs]
        inv = [1.0 / jnp.sum(x, axis=0, keepdims=True) for x in e]
        p = [e[i] * inv[i] for i in subs]
        corr = [jnp.sum(p[i] * dp[i], axis=0, keepdims=True) for i in subs]
        pb = [x.astype(BF16) for x in p]
        ds = [(p[i] * (dp[i] - corr[i])).astype(BF16) for i in subs]
        ot = [_dot(vt_sc[g, :, pl.ds(low, width)][:, :wide[i]], pb[i], 1, 0).astype(BF16) for i in subs]
        dqt = [(_dot(kt_sc[g, :, pl.ds(low, width)][:, :wide[i]], ds[i], 1, 0) * scale).astype(BF16) for i in subs]
        for i in subs:
            dv_sc[g, at[i], :] += _dot(pb[i], go[i], 1, 0)
            dk_sc[g, at[i], :] += _dot(ds[i], q[i], 1, 0)
        return [[x.T.astype(F32).reshape(chunk, per_group, head) for x in y] for y in (ot, dqt)]

    def body(width):
        low = pl.multiple_of(top - width, LANE)
        done = [one_group(g, low, width) for g in range(groups)]
        for n, out in enumerate((att_ref, dq_ref)):
            for i in subs:
                both = [done[g][n][i] for g in range(groups)]
                both = jnp.concatenate(both, 1) if groups > 1 else both[0]
                out[i * chunk:(i + 1) * chunk] = both.astype(BF16)

    for n, width in enumerate(windows):
        cond = need <= width
        if n:
            cond &= need > windows[n - 1]
        pl.when(cond)(functools.partial(body, width))

    @pl.when(step == pl.num_programs(0) - 1)
    def _():
        for i, out in enumerate(reversed(d_refs)):
            for g in range(groups):
                lanes = slice(g * head, (g + 1) * head)
                for s in range(tok // few):
                    part = slice(s * few, (s + 1) * few)
                    out[0, part, lanes] = (dk_sc[g, place(i, s), :] * scale).astype(out.dtype)
                    out[1, part, lanes] = dv_sc[g, place(i, s), :].astype(out.dtype)


def attention(queries, grad_out, kvs, lengths, place, few, block=LANE, chunk=32):
    tok, heads, head = queries.shape
    lanes = kvs[0].shape[2]
    groups = lanes // head
    span = (BACK + 1) * tok
    most = BACK * tok + block
    windows = tuple(range(LANE, most + 1, LANE))
    smem = pl.BlockSpec(memory_space=pltpu.SMEM)
    whole = pl.BlockSpec((2, tok, lanes), lambda i: (0, 0, 0))
    tall = pl.BlockSpec((block, heads, head), lambda i: (i, 0, 0))
    out = jax.ShapeDtypeStruct(queries.shape, BF16)
    share = jax.ShapeDtypeStruct((2, tok, lanes), BF16)
    own = jax.ShapeDtypeStruct((2, tok, lanes), F32)
    return pl.pallas_call(
        functools.partial(attention_kernel, tok, few, chunk, windows),
        grid=(tok // block,),
        out_shape=(out, out, own) + (share,) * BACK,
        in_specs=[smem, smem, tall, tall] + [whole] * (BACK + 1),
        out_specs=(tall, tall) + (whole,) * (BACK + 1),
        scratch_shapes=[
            pltpu.VMEM((groups, span, head), BF16),
            pltpu.VMEM((groups, span, head), BF16),
            pltpu.VMEM((groups, head, span), BF16),
            pltpu.VMEM((groups, head, span), BF16),
            pltpu.VMEM((groups, span, head), F32),
            pltpu.VMEM((groups, span, head), F32),
        ],
        compiler_params=pltpu.CompilerParams(
            dimension_semantics=("arbitrary",), vmem_limit_bytes=40 * 2**20),
        cost_estimate=pl.CostEstimate(
            flops=12 * tok * heads * 2 * tok * head, bytes_accessed=4 * tok * heads * head * 2, transcendentals=0),
        name="attention",
    )(lengths, place, queries, grad_out, *kvs)


def route(block, distance, flip):
    n, m = lax.axis_size("ctx"), lax.axis_size("head")
    if distance == 0:
        return lax.ppermute(block, "head", [(h, h ^ flip) for h in range(m)])
    to = [c ^ 1 if distance is None else (c + distance) % n for c in range(n)]
    if flip == 0:
        return lax.ppermute(block, "ctx", [(c, to[c]) for c in range(n)])
    return lax.ppermute(block, ("ctx", "head"), [(c * m + h, to[c] * m + (h ^ flip)) for c in range(n) for h in range(m)])


def relay(block, distance):
    n = lax.axis_size("ctx")
    return lax.ppermute(block, "ctx", [(i, i + distance) for i in range(0, n, 2) if 0 <= i + distance < n])


def reorder(pieces, me):
    n, bit = len(pieces), 1
    while bit < n:
        on = (me & bit) != 0
        pieces = [jnp.where(on, pieces[i ^ bit], pieces[i]) for i in range(n)]
        bit *= 2
    return pieces


def gather(keys, values, me, odd):
    n = lax.axis_size("head")
    few, kv_heads, head = keys.shape
    lanes = kv_heads // n * head
    both = jnp.stack([keys, values]).reshape(2, few, n, lanes)
    pieces = reorder([both[:, :, i] for i in range(n)], me)
    got = route(jnp.stack(pieces[1::2]), 0, 1)
    mine = [jnp.concatenate([pieces[2 * u], got[u]], 1) for u in range(n // 2)]
    def assembled(distance):
        return jnp.concatenate([x if distance == 0 and u == 0 else route(x, distance, 2 * u) for u, x in enumerate(mine)], 1)
    two, pair, own = assembled(2), assembled(None), assembled(0)
    three = route(two, 1, 0)
    one = jnp.where(odd, pair, relay(pair, 2))
    return own, one, two, three

def scatter(own, one, two, three, me, odd):
    n = lax.axis_size("head")
    few = own.shape[1] // n
    near = route(one, None, 0).astype(F32)
    far = route(three, -1, 0).astype(F32)
    two = (two.astype(F32) + far + jnp.where(odd, near, 0.0)).astype(BF16)
    own = own + jnp.where(odd, 0.0, near)
    sums = []
    for u in range(n // 2):
        at = slice(2 * u * few, 2 * (u + 1) * few)
        base = own[:, at] if u == 0 else route(own[:, at].astype(BF16), 0, 2 * u).astype(F32)
        sums.append((base + route(two[:, at], -2, 2 * u).astype(F32)).astype(BF16))
    got = route(jnp.stack([x[:, few:] for x in sums]), 0, 1)
    pieces = [x for u in range(n // 2) for x in (sums[u][:, :few], got[u])]
    return jnp.stack(reorder(pieces, me), 2)


def on_device(queries, keys, values, grad_out, lengths):
    shard = lax.axis_index("ctx").astype(jnp.int32)
    me = lax.axis_index("head").astype(jnp.int32)
    odd = shard % 2 == 1
    spans = gather(keys, values, me, odd)
    attended, d_queries, *grads = attention(
        queries, grad_out, spans, lengths, jnp.stack([shard, me]), keys.shape[0])
    d_keys, d_values = scatter(*grads, me, odd).reshape(2, *keys.shape)
    return attended, d_queries, d_keys, d_values


def solution(mesh):
    split = P("ctx", "head", None)
    fine = P(("ctx", "head"), None, None)
    return jax.shard_map(
        on_device,
        mesh=mesh,
        in_specs=(split, fine, fine, split, P()),
        out_specs=(split, split, fine, fine),
        check_vma=False,
    )
```

```python
import functools
import math
import jax
import jax.numpy as jnp
from jax import lax
from jax.experimental import pallas as pl
from jax.experimental.pallas import tpu as pltpu
from jax.sharding import PartitionSpec as P

BACK = 3
LANE = 128
F32 = jnp.float32
BF16 = jnp.bfloat16
NEG = -1e30


def _dot(a, b, ca, cb):
    return lax.dot_general(a, b, (((ca,), (cb,)), ((), ())), preferred_element_type=F32)


def windows_of(tok, block):
    return tuple(range(LANE, BACK * tok + block + 1, LANE))


def block_kernel(tok, few, chunk, first_pass, lengths_ref, place_ref, q_ref, g_ref, *refs):
    spans, refs = refs[:BACK + 1], refs[BACK + 1:]
    if first_pass:
        stat_ref, d_refs = refs[0], refs[1:2 + BACK]
        k_sc, v_sc, q_sc, g_sc, dk_sc, dv_sc = refs[2 + BACK:]
    else:
        stat_ref, att_ref, dq_ref, k_sc, v_sc, q_sc, g_sc, kt_sc, vt_sc, o_sc, dq_sc = refs
    block, heads, head = q_ref.shape
    groups = k_sc.shape[0]
    per_group = heads // groups
    rows = chunk * per_group
    subs = range(block // chunk)
    scale = head ** -0.5
    c2 = scale * math.log2(math.e)
    step = pl.program_id(0)
    base = place_ref[0] * tok
    span0 = base - BACK * tok
    docs = lengths_ref.shape[0]

    def place(i, s):
        return pl.ds(pl.multiple_of(i * tok + (place_ref[1] ^ s) * few, few), few)

    @pl.when(step == 0)
    def _():
        for i, kv in enumerate(reversed(spans)):
            for g in range(groups):
                lanes = slice(g * head, (g + 1) * head)
                for s in range(tok // few):
                    part = slice(s * few, (s + 1) * few)
                    k_sc[g, place(i, s), :] = kv[0, part, lanes]
                    v_sc[g, place(i, s), :] = kv[1, part, lanes]
                if not first_pass:
                    at = pl.ds(i * tok, tok)
                    kt_sc[g, :, at] = k_sc[g, at, :].T
                    vt_sc[g, :, at] = v_sc[g, at, :].T
        if first_pass:
            dk_sc[...] = jnp.zeros_like(dk_sc)
            dv_sc[...] = jnp.zeros_like(dv_sc)

    for g in range(groups):
        mine = slice(g * per_group, (g + 1) * per_group)
        q_sc[g] = q_ref[...].astype(F32)[:, mine, :].reshape(block * per_group, head).astype(BF16)
        g_sc[g] = g_ref[...].astype(F32)[:, mine, :].reshape(block * per_group, head).astype(BF16)
    p0 = base + step * block
    pos = [p0 + s * chunk - span0 + lax.broadcasted_iota(jnp.int32, (1, rows), 1) // per_group for s in subs]

    def add_doc(d, carry):
        begin, first, vecs = carry
        at = begin - span0
        first = jnp.where(begin <= p0, at, first)
        vecs = tuple(jnp.where(at <= pos[s], at, vecs[s]) for s in subs)
        return begin + lengths_ref[d], first, vecs

    none = jnp.zeros((1, rows), jnp.int32)
    _, first, start = lax.fori_loop(0, docs, add_doc, (jnp.int32(0), jnp.int32(0), (none,) * len(subs)))
    top = BACK * tok + (step + 1) * block
    need = top - first

    def one_group(g, low, width):
        wide = [width - (len(subs) - 1 - s) * chunk for s in subs]
        at = [pl.ds(low, w) for w in wide]
        here = [slice(i * rows, (i + 1) * rows) for i in subs]
        q = [q_sc[g, here[i], :] for i in subs]
        go = [g_sc[g, here[i], :] for i in subs]
        s = [_dot(k_sc[g, at[i], :], q[i], 1, 1) for i in subs]
        dp = [_dot(v_sc[g, at[i], :], go[i], 1, 1) for i in subs]
        masked = []
        for i in subs:
            w = wide[i]
            key = low + lax.broadcasted_iota(jnp.int32, (w, rows), 0)
            x = jnp.where(key >= start[i], s[i], NEG)
            end = jnp.where(key[w - chunk:] <= pos[i], x[w - chunk:], NEG)
            masked.append(jnp.concatenate([x[:w - chunk], end], 0) if w > chunk else end)
        if first_pass:
            m = [jnp.max(x, axis=0, keepdims=True) * c2 for x in masked]
            e = [jnp.exp2(masked[i] * c2 - m[i]) for i in subs]
            sums = [jnp.sum(x, axis=0, keepdims=True) for x in e]
            inv = [1.0 / sums[i] for i in subs]
            p = [e[i] * inv[i] for i in subs]
            corr = [jnp.sum(e[i] * dp[i], axis=0, keepdims=True) * inv[i] for i in subs]
            for i in subs:
                stat_ref[g, 0:1, here[i]] = m[i] + jnp.log2(sums[i])
                stat_ref[g, 1:2, here[i]] = corr[i]
        else:
            p = [jnp.exp2(masked[i] * c2 - stat_ref[g, 0:1, here[i]]) for i in subs]
            corr = [stat_ref[g, 1:2, here[i]] for i in subs]
        pb = [x.astype(BF16) for x in p]
        ds = [(p[i] * (dp[i] - corr[i])).astype(BF16) for i in subs]
        if first_pass:
            for i in subs:
                dv_sc[g, at[i], :] += _dot(pb[i], go[i], 1, 0)
                dk_sc[g, at[i], :] += _dot(ds[i], q[i], 1, 0)
        else:
            for i in subs:
                ot = _dot(vt_sc[g, :, pl.ds(low, width)][:, :wide[i]], pb[i], 1, 0)
                dqt = _dot(kt_sc[g, :, pl.ds(low, width)][:, :wide[i]], ds[i], 1, 0) * scale
                o_sc[g, here[i], :] = ot.astype(BF16).T
                dq_sc[g, here[i], :] = dqt.astype(BF16).T

    def body(width):
        low = pl.multiple_of(top - width, LANE)

        def go(g, _):
            one_group(g, low, width)
            return 0

        lax.fori_loop(0, groups, go, 0)

    windows = windows_of(tok, block)
    for n, width in enumerate(windows):
        cond = need <= width
        if n:
            cond &= need > windows[n - 1]
        pl.when(cond)(functools.partial(body, width))

    if not first_pass:
        for out, cols in ((att_ref, o_sc), (dq_ref, dq_sc)):
            both = [cols[g].astype(F32).reshape(block, per_group, head) for g in range(groups)]
            out[...] = (jnp.concatenate(both, 1) if groups > 1 else both[0]).astype(BF16)
        return

    @pl.when(step == pl.num_programs(0) - 1)
    def _():
        for i, out in enumerate(reversed(d_refs)):
            for g in range(groups):
                lanes = slice(g * head, (g + 1) * head)
                for s in range(tok // few):
                    part = slice(s * few, (s + 1) * few)
                    out[0, part, lanes] = (dk_sc[g, place(i, s), :] * scale).astype(out.dtype)
                    out[1, part, lanes] = dv_sc[g, place(i, s), :].astype(out.dtype)


def block_pass(queries, grad_out, kvs, lengths, place, few, stats=None, block=LANE, chunk=32):
    first_pass = stats is None
    tok, heads, head = queries.shape
    lanes = kvs[0].shape[2]
    groups = lanes // head
    span = (BACK + 1) * tok
    rows = heads // groups * block
    smem = pl.BlockSpec(memory_space=pltpu.SMEM)
    whole = pl.BlockSpec((2, tok, lanes), lambda i: (0, 0, 0))
    tall = pl.BlockSpec((block, heads, head), lambda i: (i, 0, 0))
    thin = pl.BlockSpec((groups, 2, rows), lambda i: (0, 0, i))
    stat = jax.ShapeDtypeStruct((groups, 2, heads // groups * tok), F32)
    if first_pass:
        share = jax.ShapeDtypeStruct((2, tok, lanes), BF16)
        out_shape = (stat, jax.ShapeDtypeStruct(share.shape, F32)) + (share,) * BACK
        out_specs = (thin,) + (whole,) * (BACK + 1)
        extra = [pltpu.VMEM((groups, span, head), F32)] * 2
    else:
        out_shape = (jax.ShapeDtypeStruct(queries.shape, BF16),) * 2
        out_specs = (tall, tall)
        extra = [pltpu.VMEM((groups, head, span), BF16)] * 2 + [pltpu.VMEM((groups, rows, head), BF16)] * 2
    return pl.pallas_call(
        functools.partial(block_kernel, tok, few, chunk, first_pass),
        grid=(tok // block,),
        out_shape=out_shape,
        in_specs=[smem, smem, tall, tall] + [whole] * (BACK + 1) + ([] if first_pass else [thin]),
        out_specs=out_specs,
        scratch_shapes=[
            pltpu.VMEM((groups, span, head), BF16),
            pltpu.VMEM((groups, span, head), BF16),
            pltpu.VMEM((groups, rows, head), BF16),
            pltpu.VMEM((groups, rows, head), BF16),
            *extra,
        ],
        compiler_params=pltpu.CompilerParams(
            dimension_semantics=("arbitrary",), vmem_limit_bytes=40 * 2**20),
        cost_estimate=pl.CostEstimate(
            flops=8 * tok * heads * 2 * tok * head, bytes_accessed=4 * tok * heads * head * 2, transcendentals=0),
        name="shared_gradients" if first_pass else "row_outputs",
    )(lengths, place, queries, grad_out, *kvs, *(() if first_pass else (stats,)))


def route(block, distance, flip):
    n, m = lax.axis_size("ctx"), lax.axis_size("head")
    if distance == 0:
        return lax.ppermute(block, "head", [(h, h ^ flip) for h in range(m)])
    to = [c ^ 1 if distance is None else (c + distance) % n for c in range(n)]
    if flip == 0:
        return lax.ppermute(block, "ctx", [(c, to[c]) for c in range(n)])
    return lax.ppermute(block, ("ctx", "head"), [(c * m + h, to[c] * m + (h ^ flip)) for c in range(n) for h in range(m)])


def relay(block, distance):
    n, m = lax.axis_size("ctx"), lax.axis_size("head")
    pairs = [
        (c * m + h, c * m + (h ^ 1) if c % 2 else (c + distance) % n * m + h) for c in range(n) for h in range(m)]
    return lax.ppermute(block, ("ctx", "head"), pairs)


def reorder(pieces, me):
    n, bit = len(pieces), 1
    while bit < n:
        on = (me & bit) != 0
        pieces = [jnp.where(on, pieces[i ^ bit], pieces[i]) for i in range(n)]
        bit *= 2
    return pieces


def gather(keys, values, me, odd):
    n = lax.axis_size("head")
    few, kv_heads, head = keys.shape
    lanes = kv_heads // n * head
    both = jnp.stack([keys, values]).reshape(2, few, n, lanes)
    pieces = reorder([both[:, :, i] for i in range(n)], me)
    got = route(jnp.stack(pieces[1::2]), 0, 1)
    mine = [jnp.concatenate([pieces[2 * u], got[u]], 1) for u in range(n // 2)]
    def assembled(distance):
        return jnp.concatenate([x if distance == 0 and u == 0 else route(x, distance, 2 * u) for u, x in enumerate(mine)], 1)
    two, pair, own = assembled(2), assembled(None), assembled(0)
    three = route(two, 1, 0)
    one = jnp.where(odd, pair, relay(pair, 2))
    return own, one, two, three

def scatter(own, two, near, far, me, odd):
    n = lax.axis_size("head")
    few = own.shape[1] // n
    near, far = near.astype(F32), far.astype(F32)
    two = (two.astype(F32) + far + jnp.where(odd, near, 0.0)).astype(BF16)
    own = own + jnp.where(odd, 0.0, near)
    sums = []
    for u in range(n // 2):
        at = slice(2 * u * few, 2 * (u + 1) * few)
        base = own[:, at] if u == 0 else route(own[:, at].astype(BF16), 0, 2 * u).astype(F32)
        sums.append((base + route(two[:, at], -2, 2 * u).astype(F32)).astype(BF16))
    got = route(jnp.stack([x[:, few:] for x in sums]), 0, 1)
    pieces = [x for u in range(n // 2) for x in (sums[u][:, :few], got[u])]
    return jnp.stack(reorder(pieces, me), 2)


def on_device(queries, keys, values, grad_out, lengths):
    shard = lax.axis_index("ctx").astype(jnp.int32)
    me = lax.axis_index("head").astype(jnp.int32)
    odd = shard % 2 == 1
    spans = gather(keys, values, me, odd)
    fixed = (queries, grad_out, spans, lengths, jnp.stack([shard, me]), keys.shape[0])
    stats, *grads = block_pass(*fixed)
    near, far = route(grads[1], None, 0), route(grads[3], -1, 0)
    attended, d_queries = block_pass(*fixed, stats)
    near, far, attended, d_queries = lax.optimization_barrier((near, far, attended, d_queries))
    d_keys, d_values = scatter(grads[0], grads[2], near, far, me, odd).reshape(2, *keys.shape)
    return attended, d_queries, d_keys, d_values


def solution(mesh):
    split = P("ctx", "head", None)
    fine = P(("ctx", "head"), None, None)
    return jax.shard_map(
        on_device,
        mesh=mesh,
        in_specs=(split, fine, fine, split, P()),
        out_specs=(split, split, fine, fine),
        check_vma=False,
    )
```

```python
import functools
import math
import jax
import jax.numpy as jnp
from jax import lax
from jax.experimental import pallas as pl
from jax.experimental.pallas import tpu as pltpu
from jax.sharding import PartitionSpec as P

BACK = 3
LANE = 128
F32 = jnp.float32
BF16 = jnp.bfloat16
NEG = -1e30


def _dot(a, b, ca, cb):
    return lax.dot_general(a, b, (((ca,), (cb,)), ((), ())), preferred_element_type=F32)


def windows_of(tok, block):
    return tuple(range(LANE, BACK * tok + block + 1, LANE))


def block_kernel(tok, few, chunk, first_pass, lengths_ref, place_ref, q_ref, g_ref, *refs):
    spans, refs = refs[:BACK + 1], refs[BACK + 1:]
    if first_pass:
        stat_ref, d_refs = refs[0], refs[1:2 + BACK]
        k_sc, v_sc, q_sc, g_sc, dk_sc, dv_sc = refs[2 + BACK:]
    else:
        stat_ref, att_ref, dq_ref, k_sc, v_sc, q_sc, g_sc, kt_sc, vt_sc, o_sc, dq_sc = refs
    block, heads, head = q_ref.shape
    groups = k_sc.shape[0]
    per_group = heads // groups
    rows = chunk * per_group
    subs = range(block // chunk)
    scale = head ** -0.5
    c2 = scale * math.log2(math.e)
    step = pl.program_id(0)
    base = place_ref[0] * tok
    span0 = base - BACK * tok
    docs = lengths_ref.shape[0]

    def place(i, s):
        return pl.ds(pl.multiple_of(i * tok + (place_ref[1] ^ s) * few, few), few)

    @pl.when(step == 0)
    def _():
        for i, kv in enumerate(reversed(spans)):
            for g in range(groups):
                lanes = slice(g * head, (g + 1) * head)
                for s in range(tok // few):
                    part = slice(s * few, (s + 1) * few)
                    k_sc[g, place(i, s), :] = kv[0, part, lanes]
                    v_sc[g, place(i, s), :] = kv[1, part, lanes]
                if not first_pass:
                    at = pl.ds(i * tok, tok)
                    kt_sc[g, :, at] = k_sc[g, at, :].T
                    vt_sc[g, :, at] = v_sc[g, at, :].T
        if first_pass:
            dk_sc[...] = jnp.zeros_like(dk_sc)
            dv_sc[...] = jnp.zeros_like(dv_sc)

    for g in range(groups):
        mine = slice(g * per_group, (g + 1) * per_group)
        q_sc[g] = q_ref[...].astype(F32)[:, mine, :].reshape(block * per_group, head).astype(BF16)
        g_sc[g] = g_ref[...].astype(F32)[:, mine, :].reshape(block * per_group, head).astype(BF16)
    p0 = base + step * block
    pos = [p0 + s * chunk - span0 + lax.broadcasted_iota(jnp.int32, (1, rows), 1) // per_group for s in subs]

    def add_doc(d, carry):
        begin, first, vecs = carry
        at = begin - span0
        first = jnp.where(begin <= p0, at, first)
        vecs = tuple(jnp.where(at <= pos[s], at, vecs[s]) for s in subs)
        return begin + lengths_ref[d], first, vecs

    none = jnp.zeros((1, rows), jnp.int32)
    _, first, start = lax.fori_loop(0, docs, add_doc, (jnp.int32(0), jnp.int32(0), (none,) * len(subs)))
    top = BACK * tok + (step + 1) * block
    need = top - first

    def one_group(g, low, width):
        wide = [width - (len(subs) - 1 - s) * chunk for s in subs]
        at = [pl.ds(low, w) for w in wide]
        here = [slice(i * rows, (i + 1) * rows) for i in subs]
        q = [q_sc[g, here[i], :] for i in subs]
        go = [g_sc[g, here[i], :] for i in subs]
        s = [_dot(k_sc[g, at[i], :], q[i], 1, 1) for i in subs]
        dp = [_dot(v_sc[g, at[i], :], go[i], 1, 1) for i in subs]
        masked = []
        for i in subs:
            w = wide[i]
            key = low + lax.broadcasted_iota(jnp.int32, (w, rows), 0)
            x = jnp.where(key >= start[i], s[i], NEG)
            end = jnp.where(key[w - chunk:] <= pos[i], x[w - chunk:], NEG)
            masked.append(jnp.concatenate([x[:w - chunk], end], 0) if w > chunk else end)
        if first_pass:
            m = [jnp.max(x, axis=0, keepdims=True) * c2 for x in masked]
            e = [jnp.exp2(masked[i] * c2 - m[i]) for i in subs]
            sums = [jnp.sum(x, axis=0, keepdims=True) for x in e]
            inv = [1.0 / sums[i] for i in subs]
            p = [e[i] * inv[i] for i in subs]
            corr = [jnp.sum(e[i] * dp[i], axis=0, keepdims=True) * inv[i] for i in subs]
            for i in subs:
                stat_ref[g, 0:1, here[i]] = m[i] + jnp.log2(sums[i])
                stat_ref[g, 1:2, here[i]] = corr[i]
        else:
            p = [jnp.exp2(masked[i] * c2 - stat_ref[g, 0:1, here[i]]) for i in subs]
            corr = [stat_ref[g, 1:2, here[i]] for i in subs]
        pb = [x.astype(BF16) for x in p]
        ds = [(p[i] * (dp[i] - corr[i])).astype(BF16) for i in subs]
        if first_pass:
            for i in subs:
                dv_sc[g, at[i], :] += _dot(pb[i], go[i], 1, 0)
                dk_sc[g, at[i], :] += _dot(ds[i], q[i], 1, 0)
        else:
            for i in subs:
                ot = _dot(vt_sc[g, :, pl.ds(low, width)][:, :wide[i]], pb[i], 1, 0)
                dqt = _dot(kt_sc[g, :, pl.ds(low, width)][:, :wide[i]], ds[i], 1, 0) * scale
                o_sc[g, here[i], :] = ot.astype(BF16).T
                dq_sc[g, here[i], :] = dqt.astype(BF16).T

    def body(width):
        low = pl.multiple_of(top - width, LANE)

        def go(g, _):
            one_group(g, low, width)
            return 0

        lax.fori_loop(0, groups, go, 0)

    windows = windows_of(tok, block)
    for n, width in enumerate(windows):
        cond = need <= width
        if n:
            cond &= need > windows[n - 1]
        pl.when(cond)(functools.partial(body, width))

    if not first_pass:
        for out, cols in ((att_ref, o_sc), (dq_ref, dq_sc)):
            both = [cols[g].astype(F32).reshape(block, per_group, head) for g in range(groups)]
            out[...] = (jnp.concatenate(both, 1) if groups > 1 else both[0]).astype(BF16)
        return

    @pl.when(step == pl.num_programs(0) - 1)
    def _():
        for i, out in enumerate(reversed(d_refs)):
            for g in range(groups):
                lanes = slice(g * head, (g + 1) * head)
                for s in range(tok // few):
                    part = slice(s * few, (s + 1) * few)
                    out[0, part, lanes] = (dk_sc[g, place(i, s), :] * scale).astype(out.dtype)
                    out[1, part, lanes] = dv_sc[g, place(i, s), :].astype(out.dtype)


def block_pass(queries, grad_out, kvs, lengths, place, few, stats=None, block=LANE, chunk=32):
    first_pass = stats is None
    tok, heads, head = queries.shape
    lanes = kvs[0].shape[2]
    groups = lanes // head
    span = (BACK + 1) * tok
    rows = heads // groups * block
    smem = pl.BlockSpec(memory_space=pltpu.SMEM)
    whole = pl.BlockSpec((2, tok, lanes), lambda i: (0, 0, 0))
    tall = pl.BlockSpec((block, heads, head), lambda i: (i, 0, 0))
    thin = pl.BlockSpec((groups, 2, rows), lambda i: (0, 0, i))
    stat = jax.ShapeDtypeStruct((groups, 2, heads // groups * tok), F32)
    if first_pass:
        share = jax.ShapeDtypeStruct((2, tok, lanes), BF16)
        out_shape = (stat, jax.ShapeDtypeStruct(share.shape, F32)) + (share,) * BACK
        out_specs = (thin,) + (whole,) * (BACK + 1)
        extra = [pltpu.VMEM((groups, span, head), F32)] * 2
    else:
        out_shape = (jax.ShapeDtypeStruct(queries.shape, BF16),) * 2
        out_specs = (tall, tall)
        extra = [pltpu.VMEM((groups, head, span), BF16)] * 2 + [pltpu.VMEM((groups, rows, head), BF16)] * 2
    return pl.pallas_call(
        functools.partial(block_kernel, tok, few, chunk, first_pass),
        grid=(tok // block,),
        out_shape=out_shape,
        in_specs=[smem, smem, tall, tall] + [whole] * (BACK + 1) + ([] if first_pass else [thin]),
        out_specs=out_specs,
        scratch_shapes=[
            pltpu.VMEM((groups, span, head), BF16),
            pltpu.VMEM((groups, span, head), BF16),
            pltpu.VMEM((groups, rows, head), BF16),
            pltpu.VMEM((groups, rows, head), BF16),
            *extra,
        ],
        compiler_params=pltpu.CompilerParams(
            dimension_semantics=("arbitrary",), vmem_limit_bytes=40 * 2**20),
        cost_estimate=pl.CostEstimate(
            flops=8 * tok * heads * 2 * tok * head, bytes_accessed=4 * tok * heads * head * 2, transcendentals=0),
        name="shared_gradients" if first_pass else "row_outputs",
    )(lengths, place, queries, grad_out, *kvs, *(() if first_pass else (stats,)))


def route(block, distance, flip):
    n, m = lax.axis_size("ctx"), lax.axis_size("head")
    if distance == 0:
        return lax.ppermute(block, "head", [(h, h ^ flip) for h in range(m)])
    to = [c ^ 1 if distance is None else (c + distance) % n for c in range(n)]
    if flip == 0:
        return lax.ppermute(block, "ctx", [(c, to[c]) for c in range(n)])
    return lax.ppermute(block, ("ctx", "head"), [(c * m + h, to[c] * m + (h ^ flip)) for c in range(n) for h in range(m)])


def relay(block, distance):
    n, m = lax.axis_size("ctx"), lax.axis_size("head")
    pairs = [
        (c * m + h, c * m + (h ^ 1) if c % 2 else (c + distance) % n * m + h) for c in range(n) for h in range(m)]
    return lax.ppermute(block, ("ctx", "head"), pairs)


def reorder(pieces, me):
    n, bit = len(pieces), 1
    while bit < n:
        on = (me & bit) != 0
        pieces = [jnp.where(on, pieces[i ^ bit], pieces[i]) for i in range(n)]
        bit *= 2
    return pieces


def gather(keys, values, me, shard):
    n = lax.axis_size("head")
    few, kv_heads, head = keys.shape
    lanes = kv_heads // n * head
    both = jnp.stack([keys, values]).reshape(2, few, n, lanes)
    pieces = reorder([both[:, :, i] for i in range(n)], me)
    got = route(jnp.stack(pieces[1::2]), 0, 1)
    mine = [jnp.concatenate([pieces[2 * u], got[u]], 1) for u in range(n // 2)]

    def assembled(distance):
        return jnp.concatenate([x if distance == 0 and u == 0 else route(x, distance, 2 * u) for u, x in enumerate(mine)], 1)
    odd = shard % 2 == 1
    two, pair, own = assembled(2), assembled(None), assembled(0)
    three = lax.optimization_barrier(route(two, 1, 0) * (shard >= BACK).astype(BF16))
    three = jnp.where(shard >= BACK, three, jnp.zeros_like(two))
    one = jnp.where(odd, pair, relay(pair, 2))
    return own, one, two, three

def scatter(own, two, near, far, me, odd):
    n = lax.axis_size("head")
    few = own.shape[1] // n
    near, far = near.astype(F32), far.astype(F32)
    two = (two.astype(F32) + far + jnp.where(odd, near, 0.0)).astype(BF16)
    own = own + jnp.where(odd, 0.0, near)
    sums = []
    for u in range(n // 2):
        at = slice(2 * u * few, 2 * (u + 1) * few)
        base = own[:, at] if u == 0 else route(own[:, at].astype(BF16), 0, 2 * u).astype(F32)
        sums.append((base + route(two[:, at], -2, 2 * u).astype(F32)).astype(BF16))
    got = route(jnp.stack([x[:, few:] for x in sums]), 0, 1)
    pieces = [x for u in range(n // 2) for x in (sums[u][:, :few], got[u])]
    return jnp.stack(reorder(pieces, me), 2)


def on_device(queries, keys, values, grad_out, lengths):
    shard = lax.axis_index("ctx").astype(jnp.int32)
    me = lax.axis_index("head").astype(jnp.int32)
    odd = shard % 2 == 1
    spans = gather(keys, values, me, shard)
    fixed = (queries, grad_out, spans, lengths, jnp.stack([shard, me]), keys.shape[0])
    stats, *grads = block_pass(*fixed)
    near, far = route(grads[1], None, 0), route(grads[3], -1, 0)
    attended, d_queries = block_pass(*fixed, stats)
    near, far, attended, d_queries = lax.optimization_barrier((near, far, attended, d_queries))
    d_keys, d_values = scatter(grads[0], grads[2], near, far, me, odd).reshape(2, *keys.shape)
    return attended, d_queries, d_keys, d_values


def solution(mesh):
    split = P("ctx", "head", None)
    fine = P(("ctx", "head"), None, None)
    return jax.shard_map(
        on_device,
        mesh=mesh,
        in_specs=(split, fine, fine, split, P()),
        out_specs=(split, split, fine, fine),
        check_vma=False,
    )
```

```python
import functools
import math
import jax
import jax.numpy as jnp
from jax import lax
from jax.experimental import pallas as pl
from jax.experimental.pallas import tpu as pltpu
from jax.sharding import PartitionSpec as P

BACK = 3
LANE = 128
F32 = jnp.float32
BF16 = jnp.bfloat16
NEG = -1e30


def _dot(a, b, ca, cb):
    return lax.dot_general(a, b, (((ca,), (cb,)), ((), ())), preferred_element_type=F32)


def windows_of(tok, block):
    return tuple(range(LANE, BACK * tok + block + 1, LANE))


def block_kernel(tok, few, chunk, first_pass, lengths_ref, place_ref, q_ref, g_ref, *refs):
    spans, refs = refs[:BACK + 1], refs[BACK + 1:]
    if first_pass:
        stat_ref, d_refs = refs[0], refs[1:2 + BACK]
        k_sc, v_sc, q_sc, g_sc, dk_sc, dv_sc = refs[2 + BACK:]
    else:
        stat_ref, att_ref, dq_ref, k_sc, v_sc, q_sc, g_sc, kt_sc, vt_sc, o_sc, dq_sc = refs
    block, heads, head = q_ref.shape
    groups = k_sc.shape[0]
    per_group = heads // groups
    rows = chunk * per_group
    subs = range(block // chunk)
    scale = head ** -0.5
    c2 = scale * math.log2(math.e)
    step = pl.program_id(0)
    base = place_ref[0] * tok
    span0 = base - BACK * tok
    docs = lengths_ref.shape[0]

    def place(i, s):
        return pl.ds(pl.multiple_of(i * tok + (place_ref[1] ^ s) * few, few), few)

    @pl.when(step == 0)
    def _():
        for i, kv in enumerate(reversed(spans)):
            for g in range(groups):
                lanes = slice(g * head, (g + 1) * head)
                for s in range(tok // few):
                    part = slice(s * few, (s + 1) * few)
                    k_sc[g, place(i, s), :] = kv[0, part, lanes]
                    v_sc[g, place(i, s), :] = kv[1, part, lanes]
                if not first_pass:
                    at = pl.ds(i * tok, tok)
                    kt_sc[g, :, at] = k_sc[g, at, :].T
                    vt_sc[g, :, at] = v_sc[g, at, :].T
        if first_pass:
            dk_sc[...] = jnp.zeros_like(dk_sc)
            dv_sc[...] = jnp.zeros_like(dv_sc)

    for g in range(groups):
        mine = slice(g * per_group, (g + 1) * per_group)
        q_sc[g] = q_ref[...].astype(F32)[:, mine, :].reshape(block * per_group, head).astype(BF16)
        g_sc[g] = g_ref[...].astype(F32)[:, mine, :].reshape(block * per_group, head).astype(BF16)
    p0 = base + step * block
    pos = [p0 + s * chunk - span0 + lax.broadcasted_iota(jnp.int32, (1, rows), 1) // per_group for s in subs]

    def add_doc(d, carry):
        begin, first, vecs = carry
        at = begin - span0
        first = jnp.where(begin <= p0, at, first)
        vecs = tuple(jnp.where(at <= pos[s], at, vecs[s]) for s in subs)
        return begin + lengths_ref[d], first, vecs

    none = jnp.zeros((1, rows), jnp.int32)
    _, first, start = lax.fori_loop(0, docs, add_doc, (jnp.int32(0), jnp.int32(0), (none,) * len(subs)))
    top = BACK * tok + (step + 1) * block
    need = top - first

    def one_group(g, low, width):
        wide = [width - (len(subs) - 1 - s) * chunk for s in subs]
        at = [pl.ds(low, w) for w in wide]
        here = [slice(i * rows, (i + 1) * rows) for i in subs]
        q = [q_sc[g, here[i], :] for i in subs]
        go = [g_sc[g, here[i], :] for i in subs]
        s = [_dot(k_sc[g, at[i], :], q[i], 1, 1) for i in subs]
        dp = [_dot(v_sc[g, at[i], :], go[i], 1, 1) for i in subs]
        masked = []
        for i in subs:
            w = wide[i]
            key = low + lax.broadcasted_iota(jnp.int32, (w, rows), 0)
            x = jnp.where(key >= start[i], s[i], NEG)
            end = jnp.where(key[w - chunk:] <= pos[i], x[w - chunk:], NEG)
            masked.append(jnp.concatenate([x[:w - chunk], end], 0) if w > chunk else end)
        if first_pass:
            m = [jnp.max(x, axis=0, keepdims=True) * c2 for x in masked]
            e = [jnp.exp2(masked[i] * c2 - m[i]) for i in subs]
            sums = [jnp.sum(x, axis=0, keepdims=True) for x in e]
            inv = [1.0 / sums[i] for i in subs]
            p = [e[i] * inv[i] for i in subs]
            corr = [jnp.sum(e[i] * dp[i], axis=0, keepdims=True) * inv[i] for i in subs]
            for i in subs:
                stat_ref[g, 0:1, here[i]] = m[i] + jnp.log2(sums[i])
                stat_ref[g, 1:2, here[i]] = corr[i]
        else:
            p = [jnp.exp2(masked[i] * c2 - stat_ref[g, 0:1, here[i]]) for i in subs]
            corr = [stat_ref[g, 1:2, here[i]] for i in subs]
        pb = [x.astype(BF16) for x in p]
        ds = [(p[i] * (dp[i] - corr[i])).astype(BF16) for i in subs]
        if first_pass:
            for i in subs:
                dv_sc[g, at[i], :] += _dot(pb[i], go[i], 1, 0)
                dk_sc[g, at[i], :] += _dot(ds[i], q[i], 1, 0)
        else:
            for i in subs:
                ot = _dot(vt_sc[g, :, pl.ds(low, width)][:, :wide[i]], pb[i], 1, 0)
                dqt = _dot(kt_sc[g, :, pl.ds(low, width)][:, :wide[i]], ds[i], 1, 0) * scale
                o_sc[g, here[i], :] = ot.astype(BF16).T
                dq_sc[g, here[i], :] = dqt.astype(BF16).T

    def body(width):
        low = pl.multiple_of(top - width, LANE)

        def go(g, _):
            one_group(g, low, width)
            return 0

        lax.fori_loop(0, groups, go, 0)

    windows = windows_of(tok, block)
    for n, width in enumerate(windows):
        cond = need <= width
        if n:
            cond &= need > windows[n - 1]
        pl.when(cond)(functools.partial(body, width))

    if not first_pass:
        for out, cols in ((att_ref, o_sc), (dq_ref, dq_sc)):
            both = [cols[g].astype(F32).reshape(block, per_group, head) for g in range(groups)]
            out[...] = (jnp.concatenate(both, 1) if groups > 1 else both[0]).astype(BF16)
        return

    @pl.when(step == pl.num_programs(0) - 1)
    def _():
        for i, out in enumerate(reversed(d_refs)):
            for g in range(groups):
                lanes = slice(g * head, (g + 1) * head)
                for s in range(tok // few):
                    part = slice(s * few, (s + 1) * few)
                    out[0, part, lanes] = (dk_sc[g, place(i, s), :] * scale).astype(out.dtype)
                    out[1, part, lanes] = dv_sc[g, place(i, s), :].astype(out.dtype)


def block_pass(queries, grad_out, kvs, lengths, place, few, stats=None, block=LANE, chunk=32):
    first_pass = stats is None
    tok, heads, head = queries.shape
    lanes = kvs[0].shape[2]
    groups = lanes // head
    span = (BACK + 1) * tok
    rows = heads // groups * block
    smem = pl.BlockSpec(memory_space=pltpu.SMEM)
    whole = pl.BlockSpec((2, tok, lanes), lambda i: (0, 0, 0))
    tall = pl.BlockSpec((block, heads, head), lambda i: (i, 0, 0))
    thin = pl.BlockSpec((groups, 2, rows), lambda i: (0, 0, i))
    stat = jax.ShapeDtypeStruct((groups, 2, heads // groups * tok), F32)
    if first_pass:
        share = jax.ShapeDtypeStruct((2, tok, lanes), BF16)
        out_shape = (stat, jax.ShapeDtypeStruct(share.shape, F32)) + (share,) * BACK
        out_specs = (thin,) + (whole,) * (BACK + 1)
        extra = [pltpu.VMEM((groups, span, head), F32)] * 2
    else:
        out_shape = (jax.ShapeDtypeStruct(queries.shape, BF16),) * 2
        out_specs = (tall, tall)
        extra = [pltpu.VMEM((groups, head, span), BF16)] * 2 + [pltpu.VMEM((groups, rows, head), BF16)] * 2
    return pl.pallas_call(
        functools.partial(block_kernel, tok, few, chunk, first_pass),
        grid=(tok // block,),
        out_shape=out_shape,
        in_specs=[smem, smem, tall, tall] + [whole] * (BACK + 1) + ([] if first_pass else [thin]),
        out_specs=out_specs,
        scratch_shapes=[
            pltpu.VMEM((groups, span, head), BF16),
            pltpu.VMEM((groups, span, head), BF16),
            pltpu.VMEM((groups, rows, head), BF16),
            pltpu.VMEM((groups, rows, head), BF16),
            *extra,
        ],
        compiler_params=pltpu.CompilerParams(
            dimension_semantics=("arbitrary",), vmem_limit_bytes=40 * 2**20),
        cost_estimate=pl.CostEstimate(
            flops=8 * tok * heads * 2 * tok * head, bytes_accessed=4 * tok * heads * head * 2, transcendentals=0),
        name="shared_gradients" if first_pass else "row_outputs",
    )(lengths, place, queries, grad_out, *kvs, *(() if first_pass else (stats,)))


def route(block, distance, flip):
    n, m = lax.axis_size("ctx"), lax.axis_size("head")
    if distance == 0:
        return lax.ppermute(block, "head", [(h, h ^ flip) for h in range(m)])
    to = [c ^ 1 if distance is None else (c + distance) % n for c in range(n)]
    if flip == 0:
        return lax.ppermute(block, "ctx", [(c, to[c]) for c in range(n)])
    return lax.ppermute(block, ("ctx", "head"), [(c * m + h, to[c] * m + (h ^ flip)) for c in range(n) for h in range(m)])


def relay(block, distance):
    n, m = lax.axis_size("ctx"), lax.axis_size("head")
    pairs = [
        (c * m + h, c * m + (h ^ 1) if c % 2 else (c + distance) % n * m + h) for c in range(n) for h in range(m)]
    return lax.ppermute(block, ("ctx", "head"), pairs)


def reorder(pieces, me):
    n, bit = len(pieces), 1
    while bit < n:
        on = (me & bit) != 0
        pieces = [jnp.where(on, pieces[i ^ bit], pieces[i]) for i in range(n)]
        bit *= 2
    return pieces


def gather(keys, values, me, shard):
    n = lax.axis_size("head")
    few, kv_heads, head = keys.shape
    lanes = kv_heads // n * head
    both = jnp.stack([keys.reshape(few, n, lanes).transpose(1, 0, 2), values.reshape(few, n, lanes).transpose(1, 0, 2)], 1)
    pieces = reorder([both[i] for i in range(n)], me)
    got = route(jnp.stack(pieces[1::2]), 0, 1)
    mine = [jnp.concatenate([pieces[2 * u], got[u]], 1) for u in range(n // 2)]

    def assembled(distance):
        return jnp.concatenate([x if distance == 0 and u == 0 else route(x, distance, 2 * u) for u, x in enumerate(mine)], 1)
    odd = shard % 2 == 1
    two, pair, own = assembled(2), assembled(None), assembled(0)
    three = lax.optimization_barrier(route(two, 1, 0) * (shard >= BACK).astype(BF16))
    three = jnp.where(shard >= BACK, three, jnp.zeros_like(two))
    one = jnp.where(odd, pair, relay(pair, 2))
    return own, one, two, three

def scatter(own, two, near, far, me, odd):
    n = lax.axis_size("head")
    few = own.shape[1] // n
    near, far = near.astype(F32), far.astype(F32)
    two = (two.astype(F32) + far + jnp.where(odd, near, 0.0)).astype(BF16)
    own = own + jnp.where(odd, 0.0, near)
    sums = []
    for u in range(n // 2):
        at = slice(2 * u * few, 2 * (u + 1) * few)
        base = own[:, at] if u == 0 else route(own[:, at].astype(BF16), 0, 2 * u).astype(F32)
        sums.append((base + route(two[:, at], -2, 2 * u).astype(F32)).astype(BF16))
    got = route(jnp.stack([x[:, few:] for x in sums]), 0, 1)
    pieces = [x for u in range(n // 2) for x in (sums[u][:, :few], got[u])]
    return jnp.stack(reorder(pieces, me), 2)


def on_device(queries, keys, values, grad_out, lengths):
    shard = lax.axis_index("ctx").astype(jnp.int32)
    me = lax.axis_index("head").astype(jnp.int32)
    odd = shard % 2 == 1
    spans = gather(keys, values, me, shard)
    fixed = (queries, grad_out, spans, lengths, jnp.stack([shard, me]), keys.shape[0])
    stats, *grads = block_pass(*fixed)
    near, far = route(grads[1], None, 0), route(grads[3], -1, 0)
    attended, d_queries = block_pass(*fixed, stats)
    near, far, attended, d_queries = lax.optimization_barrier((near, far, attended, d_queries))
    d_keys, d_values = scatter(grads[0], grads[2], near, far, me, odd).reshape(2, *keys.shape)
    return attended, d_queries, d_keys, d_values


def solution(mesh):
    split = P("ctx", "head", None)
    fine = P(("ctx", "head"), None, None)
    return jax.shard_map(
        on_device,
        mesh=mesh,
        in_specs=(split, fine, fine, split, P()),
        out_specs=(split, split, fine, fine),
        check_vma=False,
    )
```
